32 devices in a mesh: ta: 4 (over y, x), gy: 8 (over z, core).
Axes of the slice: x: 2, y: 2, z: 4, core: 2. Of those that a mesh axis runs over, the one named last changes fastest.
Arguments:
- forcing: float32 [128, 512, 512], P('ta', 'gy'), may hold values from -6 to 6
- initial: float32 [128, 512, 512], P('ta', 'gy'), may hold values from -6 to 6
- class_map: int32 [512, 512], P('gy'), may hold values from 0 to 15
- speeds: float32 [16], replicated, may hold values from 0.4 to 0.65
Outputs:
- adjoint: float32 [128, 512, 512], P('ta', 'gy')
The draws below stay inside these ranges and needn't reach their ends.
All inputs are finite; a program needn't handle non-finite values.
Results may differ from the reference program's by a relative error of at most 0.0006.
Values sent between devices are 32-bit elements; how exact they have to be, the bound alone decides.
A program may use at most 128 MiB of HBM per device.

```python
import jax
import jax.numpy as jnp
from jax import lax

NX = 512
NY = 512
ITERS = 2
CLASSES = 16
NT = 128


def draw_forcing(key, part):
    keys = jax.random.split(key, 4)
    moments = jnp.arange(NT, dtype=jnp.int32).astype(jnp.float32)
    row_pos = jnp.arange(NY, dtype=jnp.int32).astype(jnp.float32)
    col_pos = jnp.arange(NX, dtype=jnp.int32).astype(jnp.float32)
    envelope = jnp.sin(jnp.pi * (row_pos + 0.5) / NY)[None, :, None]
    still_periods = jnp.array([4.5, 4.8, 5.1, 5.4, 5.7], jnp.float32)
    still_phase = jax.random.uniform(keys[0], (5,), jnp.float32, 0.0, 2.0 * jnp.pi)
    still = jnp.sum(jnp.cos(2.0 * jnp.pi * col_pos[None, :] / still_periods[:, None] + still_phase[:, None]), axis=0)
    wave_periods = jnp.array([9.5, 10.5, 11.5, 12.5], jnp.float32)
    beat_periods = 1.9 * wave_periods
    wave_phase = jax.random.uniform(keys[1], (4,), jnp.float32, 0.0, 2.0 * jnp.pi)
    beat_phase = jax.random.uniform(keys[2], (4,), jnp.float32, 0.0, 2.0 * jnp.pi)
    across = jnp.cos(2.0 * jnp.pi * col_pos[None, :] / wave_periods[:, None] + wave_phase[:, None])
    along = jnp.cos(2.0 * jnp.pi * moments[None, :] / beat_periods[:, None] + beat_phase[:, None])
    travel = across[:, None, :] * along[:, :, None]
    travel = travel[0] + travel[1] + travel[2] + travel[3]
    noise = 0.3 * jax.random.truncated_normal(keys[3], -4.0, 4.0, (NT, NY, NX), jnp.float32)
    field = envelope * (0.8 * still[None, None, :] + 0.5 * travel[:, None, :]) + noise
    return jnp.clip(field, -6.0, 6.0)


def place_ends(drawn, stream_key, least, largest):
    dims = drawn.shape
    spot = [jax.random.randint(jax.random.fold_in(stream_key, axis), (), 0, dims[axis]) for axis in range(len(dims))]
    drawn = drawn.at[tuple(spot)].set(least)
    longest = dims.index(max(dims))
    spot[longest] = (spot[longest] + 1) % dims[longest]
    return drawn.at[tuple(spot)].set(largest)


def level_of(own_key, dims, cuts, low, largest):
    loudness, own = 1.0, jax.random.fold_in(own_key, 6)
    for axis_at, shards_of in cuts:
        draws = jnp.exp(jax.random.uniform(jax.random.fold_in(own, axis_at), (shards_of,), jnp.float32, low / len(cuts), largest / len(cuts)))
        loudness = loudness * jnp.repeat(draws, dims[axis_at] // shards_of).reshape([-1 if axis == axis_at else 1 for axis in range(len(dims))])
    return loudness


def scatter_about(key, dims, scale, most, shards=(), kind=jnp.bfloat16):
    values = jax.random.normal(key, dims, jnp.float32) * scale
    if len(shards) > 0:
        values = level_of(key, dims, shards, -0.22, 0.18) * values
    return jnp.clip(values, min=-most, max=most).astype(kind)


def setup_inputs(seed: int = 0) -> dict:
    arg_keys = jax.random.split(jax.random.key(seed), 5)
    return {
        "forcing": draw_forcing(jax.random.fold_in(arg_keys[4], 71), 0),
        "initial": scatter_about(arg_keys[1], (NT, NY, NX), 1.0, 6.0, ((0, 4), (1, 8)), jnp.float32),
        "class_map": place_ends(jax.random.randint(arg_keys[2], (NY, NX), 0, CLASSES), jax.random.fold_in(arg_keys[2], 1), 0, CLASSES - 1).astype(jnp.int32),
        "speeds": jnp.clip(jax.random.uniform(arg_keys[3], (CLASSES,), jnp.float32, 0.4, 0.65), 0.4, 0.65),
    }


damping = 0.2
wrap_factor = 0.01

def sine_table(length, row_order):
    modes = jnp.arange(length, dtype=jnp.int32)
    phase = (modes[:, None] + 1) * (row_order[None, :] + 1) % (2 * length + 2)
    angle = jnp.pi * phase.astype(jnp.float32) / (length + 1)
    return jnp.sqrt(2.0 / (length + 1)) * jnp.sin(angle)

def time_tables(all_steps):
    slots = jnp.arange(all_steps // 2, dtype=jnp.int32)[:, None]
    moments = jnp.arange(all_steps, dtype=jnp.int32)[None, :]
    angle = 2.0 * jnp.pi / all_steps * (slots * moments % all_steps).astype(jnp.float32)
    parity = (1 - 2 * (moments % 2)).astype(jnp.float32)
    first = slots == 0
    cos_table = jnp.cos(angle) + jnp.zeros_like(parity)
    sin_table = jnp.where(first, parity, -jnp.sin(angle))
    cos_inverse = jnp.where(first, 1.0, 2.0) * jnp.cos(angle) / all_steps
    sin_inverse = jnp.where(first, parity, -2.0 * jnp.sin(angle)) / all_steps
    return (cos_table, sin_table, cos_inverse, sin_inverse)

def symbol_factors(slot_start, slot_count, all_steps, row_count, col_count, mean_sq):
    slots = slot_start + jnp.arange(slot_count, dtype=jnp.int32)
    phase = (2.0 * jnp.pi / all_steps * slots.astype(jnp.float32))[:, None, None]
    log_rate = jnp.log(wrap_factor) / all_steps
    factor = jnp.exp(log_rate)
    gap = -jnp.expm1(log_rate)
    wave_real = gap + 2.0 * factor * jnp.sin(0.5 * phase) ** 2
    wave_imag = -factor * jnp.sin(phase)
    row_index = jnp.arange(row_count, dtype=jnp.int32).astype(jnp.float32)
    col_index = jnp.arange(col_count, dtype=jnp.int32).astype(jnp.float32)
    row_sigma = 4.0 * jnp.sin(jnp.pi * (row_index + 1.0) / (2.0 * row_count + 2.0)) ** 2
    col_sigma = 4.0 * jnp.sin(jnp.pi * (col_index + 1.0) / (2.0 * col_count + 2.0)) ** 2
    spatial = mean_sq * (row_sigma[None, :, None] + col_sigma[None, None, :])
    sym_real = wave_real * wave_real - wave_imag * wave_imag + damping * wave_real + spatial
    sym_imag = wave_imag * (2.0 * wave_real + damping)
    norm_sq = sym_real * sym_real + sym_imag * sym_imag
    high_mode = (1.0 + factor) ** 2 + damping * (1.0 + factor) + spatial
    first = (slots == 0)[:, None, None]
    keep_real = sym_real / norm_sq
    cross_real = sym_imag / norm_sq
    cross_imag = -sym_imag / norm_sq
    keep_imag = jnp.where(first, 1.0 / high_mode, keep_real)
    return (keep_real, cross_real, cross_imag, keep_imag)

def apply_adjoint(field, speed_field):
    extended = jnp.concatenate([field, jnp.zeros((2,) + field.shape[1:], field.dtype)], 0)
    weighted = speed_field[None] * field
    padded = jnp.pad(weighted, ((0, 0), (1, 1), (1, 1)))
    stiff = 4.0 * weighted - padded[:, :-2, 1:-1] - padded[:, 2:, 1:-1] - padded[:, 1:-1, :-2] - padded[:, 1:-1, 2:]
    return (1.0 + damping) * field - (2.0 + damping) * extended[1:-1] + extended[2:] + stiff

def precondition(resid, mean_sq):
    all_steps, row_count, col_count = resid.shape
    moments = jnp.arange(all_steps, dtype=jnp.int32).astype(jnp.float32)
    log_rate = jnp.log(wrap_factor) / all_steps
    grow_scale = jnp.exp(-moments * log_rate)[:, None, None]
    shrink_scale = jnp.exp(moments * log_rate)[:, None, None]
    x_table = sine_table(col_count, jnp.arange(col_count, dtype=jnp.int32))
    y_table = sine_table(row_count, jnp.arange(row_count, dtype=jnp.int32))
    cos_table, sin_table, cos_inverse, sin_inverse = time_tables(all_steps)
    scaled = resid * grow_scale
    x_modes = jnp.dot(scaled.reshape(-1, col_count), x_table, precision=lax.Precision.HIGHEST, preferred_element_type=jnp.float32).reshape(resid.shape)
    merged = x_modes.reshape(all_steps, -1)
    half_shape = (all_steps // 2, row_count, col_count)
    time_real = jnp.dot(cos_table, merged, precision=lax.Precision.HIGHEST, preferred_element_type=jnp.float32).reshape(half_shape)
    time_imag = jnp.dot(sin_table, merged, precision=lax.Precision.HIGHEST, preferred_element_type=jnp.float32).reshape(half_shape)
    y_real = jnp.einsum('lp,kpx->klx', y_table, time_real, precision=lax.Precision.HIGHEST, preferred_element_type=jnp.float32)
    y_imag = jnp.einsum('lp,kpx->klx', y_table, time_imag, precision=lax.Precision.HIGHEST, preferred_element_type=jnp.float32)
    keep_real, cross_real, cross_imag, keep_imag = symbol_factors(0, all_steps // 2, all_steps, row_count, col_count, mean_sq)
    div_real = y_real * keep_real + y_imag * cross_real
    div_imag = y_real * cross_imag + y_imag * keep_imag
    back_real = jnp.einsum('lp,klx->kpx', y_table, div_real, precision=lax.Precision.HIGHEST, preferred_element_type=jnp.float32)
    back_imag = jnp.einsum('lp,klx->kpx', y_table, div_imag, precision=lax.Precision.HIGHEST, preferred_element_type=jnp.float32)
    timed = jnp.dot(cos_inverse.T, back_real.reshape(all_steps // 2, -1), precision=lax.Precision.HIGHEST, preferred_element_type=jnp.float32)
    timed = timed + jnp.dot(sin_inverse.T, back_imag.reshape(all_steps // 2, -1), precision=lax.Precision.HIGHEST, preferred_element_type=jnp.float32)
    result = jnp.dot(timed.reshape(-1, col_count), x_table, precision=lax.Precision.HIGHEST, preferred_element_type=jnp.float32).reshape(resid.shape)
    return result * shrink_scale

def reference(forcing, initial, class_map, speeds):
    speed_sq = speeds * speeds
    mean_sq = jnp.mean(speed_sq)
    speed_field = speed_sq[class_map]
    adjoint = initial
    for sweep in range(ITERS):
        resid = forcing - apply_adjoint(adjoint, speed_field)
        adjoint = adjoint + precondition(resid, mean_sq)
    return adjoint
```

```python
import functools

import jax
import jax.numpy as jnp
import numpy as np
from jax import lax
from jax.experimental import pallas as pl
from jax.experimental.pallas import tpu as pltpu
from jax.sharding import PartitionSpec as P

ITERS = 2


damping = 0.2
wrap_factor = 0.01
FINE = lax.Precision.HIGHEST
MID = lax.Precision.HIGH


def dot(subscripts, left, right, precision):
    return jnp.einsum(
        subscripts, left, right, precision=precision, preferred_element_type=jnp.float32
    )


def passed_along(value, axis, by):
    length = lax.axis_size(axis)
    pairs = [(i, i + by) for i in range(length) if 0 <= i + by < length]
    return lax.ppermute(value, axis, pairs)


def sine_rows(length, rows):
    modes = np.arange(length, dtype=np.int64)
    phase = (modes[:, None] + 1) * (rows[None, :] + 1) % (2 * length + 2)
    return np.sqrt(2.0 / (length + 1)) * np.sin(np.pi * phase / (length + 1))


def sigma_of(length):
    return 4.0 * np.sin(np.pi * (np.arange(length) + 1.0) / (2.0 * length + 2.0)) ** 2


def time_tables(all_steps):
    slots = np.arange(all_steps // 2, dtype=np.int64)[:, None]
    moments = np.arange(all_steps, dtype=np.int64)[None, :]
    angle = 2.0 * np.pi / all_steps * (slots * moments % all_steps)
    parity = 1.0 - 2.0 * (moments % 2)
    first = slots == 0
    forward = np.concatenate([np.cos(angle), np.where(first, parity, -np.sin(angle))], 0)
    weight = np.where(first, 1.0, 2.0)
    inverse = np.concatenate(
        [weight * np.cos(angle), np.where(first, parity, -2.0 * np.sin(angle))], 0
    )
    rate = wrap_factor ** (np.arange(all_steps) / all_steps)
    return forward / rate[None, :], (inverse / all_steps).T * rate[:, None]


def matmul_2(left, right):
    a, b, c, d = left
    e, f, g, h = right
    return (a * e + b * g, a * f + b * h, c * e + d * g, c * f + d * h)


def power_2(base, count):
    result = None
    while count:
        if count & 1:
            result = base if result is None else matmul_2(result, base)
        count >>= 1
        if count:
            base = matmul_2(base, base)
    return result


def outgoing_kernel(steps, lines, r_ref, c_ref, o_ref):
    def chunk(i, carry):
        at = pl.ds(pl.multiple_of(i * lines, lines), lines)
        c = c_ref[at, :]
        ahead = jnp.zeros_like(c)
        further = jnp.zeros_like(c)
        for n in reversed(range(steps)):
            now = c * (r_ref[n, at, :] + (2.0 + damping) * ahead - further)
            ahead, further = now, ahead
        o_ref[0, at, :] = ahead
        o_ref[1, at, :] = further
        return carry

    lax.fori_loop(0, c_ref.shape[0] // lines, chunk, 0)


def march_kernel(steps, lines, r_ref, c_ref, s_ref, v_ref):
    def chunk(i, carry):
        at = pl.ds(pl.multiple_of(i * lines, lines), lines)
        c = c_ref[at, :]
        ahead = s_ref[0, at, :]
        further = s_ref[1, at, :]
        for n in reversed(range(steps)):
            now = c * (r_ref[n, at, :] + (2.0 + damping) * ahead - further)
            v_ref[n, at, :] = now
            ahead, further = now, ahead
        return carry

    lax.fori_loop(0, c_ref.shape[0] // lines, chunk, 0)


def in_vmem(count):
    return [pl.BlockSpec(memory_space=pltpu.VMEM)] * count


def outgoing(forced, mode_scale):
    steps, rows, cols = forced.shape
    return pl.pallas_call(
        functools.partial(outgoing_kernel, steps, 8),
        out_shape=jax.ShapeDtypeStruct((2, rows, cols), jnp.float32),
        in_specs=in_vmem(2),
        out_specs=in_vmem(1)[0],
        compiler_params=pltpu.CompilerParams(vmem_limit_bytes=32 * 2**20),
    )(forced, mode_scale)


def march(forced, mode_scale, state):
    steps, rows, cols = forced.shape
    return pl.pallas_call(
        functools.partial(march_kernel, steps, 8),
        out_shape=jax.ShapeDtypeStruct((steps, rows, cols), jnp.float32),
        in_specs=in_vmem(3),
        out_specs=in_vmem(1)[0],
        compiler_params=pltpu.CompilerParams(vmem_limit_bytes=32 * 2**20),
    )(forced, mode_scale, state)


def f32(table):
    return jnp.asarray(np.asarray(table, np.float32))


def body(forcing, initial, class_map, speeds):
    steps, rows, cols = forcing.shape
    time_devices = lax.axis_size("ta")
    row_devices = lax.axis_size("gy")
    parts = time_devices * row_devices
    all_steps = steps * time_devices
    all_rows = rows * row_devices
    take = cols // parts
    slots = all_steps // 2
    edges = 2 * row_devices
    time_rank = lax.axis_index("ta")
    row_rank = lax.axis_index("gy")
    flat_rank = time_rank * row_devices + row_rank
    speed_sq = speeds * speeds
    mean_sq = jnp.mean(speed_sq)
    labels = jnp.arange(speeds.shape[0], dtype=jnp.int32)[:, None, None]
    speed_field = jnp.sum(
        jnp.where(class_map[None] == labels, speed_sq[:, None, None], 0.0), axis=0
    )

    x_table = f32(sine_rows(cols, np.arange(cols)))
    block_sine = sine_rows(rows, np.arange(rows))
    block_table = f32(block_sine)
    edge_modes = f32(block_sine[[0, rows - 1], :])
    forward, inverse = time_tables(all_steps)
    forward, inverse = f32(forward), f32(inverse)
    across = np.zeros((all_rows, row_devices, 2))
    whole = sine_rows(all_rows, np.arange(all_rows))
    for g in range(row_devices):
        if g > 0:
            across[:, g - 1, 1] = whole[:, g * rows]
        if g < row_devices - 1:
            across[:, g + 1, 0] = whole[:, (g + 1) * rows - 1]
    across = f32(across.reshape(all_rows, edges))

    mode_scale = 1.0 / (
        1.0 + damping + mean_sq * f32(sigma_of(rows)[:, None] + sigma_of(cols)[None, :])
    )
    one, none = jnp.ones_like(mode_scale), jnp.zeros_like(mode_scale)
    carried = power_2(((2.0 + damping) * mode_scale, -mode_scale, one, none), steps)
    round_trip = power_2(carried, time_devices)
    ra, rb, rc, rd = [wrap_factor * entry for entry in round_trip]
    det = (1.0 - ra) * (1.0 - rd) - rb * rc
    closing = ((1.0 - rd) / det, rb / det, rc / det, (1.0 - ra) / det)

    log_rate = np.log(wrap_factor) / all_steps
    factor = np.exp(log_rate)
    phase = 2.0 * np.pi / all_steps * np.arange(slots)
    wave_real = -np.expm1(log_rate) + 2.0 * factor * np.sin(0.5 * phase) ** 2
    wave_imag = -factor * np.sin(phase)
    base_real = np.repeat(
        wave_real * wave_real - wave_imag * wave_imag + damping * wave_real, take
    )
    base_imag = np.repeat(wave_imag * (2.0 * wave_real + damping), take)
    high = (1.0 + factor) ** 2 + damping * (1.0 + factor)
    col_index = (flat_rank * take + jnp.arange(take, dtype=jnp.int32)).astype(jnp.float32)
    col_sigma = 4.0 * jnp.sin(jnp.pi * (col_index + 1.0) / (2.0 * cols + 2.0)) ** 2
    col_sigma = jnp.tile(col_sigma, slots)
    spatial = mean_sq * (f32(sigma_of(all_rows))[:, None] + col_sigma[None, :])
    sym_real = f32(base_real)[None, :] + spatial
    sym_imag = f32(base_imag)[None, :]
    norm_sq = sym_real * sym_real + sym_imag * sym_imag
    scale_sq = mean_sq * mean_sq
    keep_real = scale_sq * sym_real / norm_sq
    cross = scale_sq * sym_imag / norm_sq
    is_first = jnp.arange(slots * take)[None, :] < take
    keep_imag = jnp.where(is_first, scale_sq / (high + spatial), keep_real)

    def incoming(out_state):
        gathered = lax.all_gather(out_state, "ta", axis=0, tiled=False)
        a, b, c, d = carried
        first = second = None
        for i in reversed(range(time_devices)):
            place = time_rank + 1 + i
            weight = jnp.where(place >= time_devices, wrap_factor, 1.0)
            part = lax.dynamic_index_in_dim(
                gathered, place % time_devices, 0, keepdims=False
            )
            part = weight * part
            if first is None:
                first, second = part[0], part[1]
            else:
                first, second = part[0] + a * first + b * second, part[1] + c * first + d * second
        a, b, c, d = closing
        return jnp.stack([a * first + b * second, c * first + d * second])

    adjoint = initial
    for sweep in range(ITERS):
        following = passed_along(adjoint[:2], "ta", -1)
        extended = jnp.concatenate([adjoint, following], 0)
        weighted = speed_field[None] * adjoint
        above = passed_along(weighted[:, -1:], "gy", 1)
        below = passed_along(weighted[:, :1], "gy", -1)
        padded = jnp.concatenate([above, weighted, below], axis=1)
        padded = jnp.pad(padded, ((0, 0), (0, 0), (1, 1)))
        stiff = (
            4.0 * weighted
            - padded[:, :-2, 1:-1]
            - padded[:, 2:, 1:-1]
            - padded[:, 1:-1, :-2]
            - padded[:, 1:-1, 2:]
        )
        applied = (
            (1.0 + damping) * adjoint - (2.0 + damping) * extended[1:-1] + extended[2:] + stiff
        )
        resid = forcing - applied
        x_modes = dot("ax,xj->aj", resid.reshape(-1, cols), x_table, MID).reshape(resid.shape)
        modes = dot("lp,npj->nlj", block_table, x_modes, MID)

        state = incoming(outgoing(modes, mode_scale))
        alone = march(modes, mode_scale, state)
        edge = dot("el,nlj->nej", edge_modes, alone, FINE)

        sent = edge.reshape(steps, 2, parts, take).transpose(2, 0, 1, 3).reshape(parts, -1)
        got = lax.all_to_all(sent, ("ta", "gy"), split_axis=0, concat_axis=0, tiled=True)
        got = got.reshape(time_devices, row_devices, steps, 2, take)
        got = got.transpose(0, 2, 1, 3, 4).reshape(all_steps, row_devices, 2, take)
        slotted = dot("kn,na->ka", forward, got.reshape(all_steps, -1), FINE)
        slotted = slotted.reshape(2 * slots, edges, take).transpose(1, 0, 2)
        rowed = dot("le,ea->la", across, slotted.reshape(edges, -1), FINE)
        row_real, row_imag = rowed[:, : slots * take], rowed[:, slots * take :]
        div = jnp.concatenate(
            [row_real * keep_real + row_imag * cross, row_imag * keep_imag - row_real * cross],
            axis=1,
        )
        back = dot("le,la->ea", across, div, FINE)
        back = back.reshape(edges, 2 * slots, take).transpose(1, 0, 2).reshape(2 * slots, -1)
        change = dot("nk,ka->na", inverse, back, FINE).reshape(got.shape)
        blank = jnp.zeros_like(got[:, :1, 0])
        beside = jnp.stack(
            [
                jnp.concatenate([blank, got[:, :-1, 1]], axis=1),
                jnp.concatenate([got[:, 1:, 0], blank], axis=1),
            ],
            axis=2,
        )
        coupled = mean_sq * beside + change
        sent = coupled.reshape(time_devices, steps, row_devices, 2, take)
        sent = sent.transpose(0, 2, 1, 3, 4).reshape(parts, -1)
        got = lax.all_to_all(sent, ("ta", "gy"), split_axis=0, concat_axis=0, tiled=True)
        coupled = got.reshape(parts, steps, 2, take).transpose(1, 2, 0, 3).reshape(steps, 2, cols)

        modes = modes + dot("el,nej->nlj", edge_modes, coupled, FINE)
        state = incoming(outgoing(modes, mode_scale))
        solved = march(modes, mode_scale, state)
        solved = dot("lp,nlj->npj", block_table, solved, MID)
        correction = dot("aj,jx->ax", solved.reshape(-1, cols), x_table, MID)
        adjoint = adjoint + correction.reshape(adjoint.shape)
    return adjoint


def solution(mesh):
    return jax.shard_map(
        body,
        mesh=mesh,
        in_specs=(P("ta", "gy", None), P("ta", "gy", None), P("gy", None), P()),
        out_specs=P("ta", "gy", None),
        check_vma=False,
    )
```

```python
import functools

import jax
import jax.numpy as jnp
import numpy as np
from jax import lax
from jax.experimental import pallas as pl
from jax.experimental.pallas import tpu as pltpu
from jax.sharding import PartitionSpec as P

ITERS = 2


damping = 0.2
wrap_factor = 0.01
FINE = lax.Precision.HIGHEST
MID = lax.Precision.HIGH


def dot(subscripts, left, right, precision):
    return jnp.einsum(
        subscripts, left, right, precision=precision, preferred_element_type=jnp.float32
    )


def passed_along(value, axis, by):
    length = lax.axis_size(axis)
    pairs = [(i, i + by) for i in range(length) if 0 <= i + by < length]
    return lax.ppermute(value, axis, pairs)


def sine_rows(length, rows):
    modes = np.arange(length, dtype=np.int64)
    phase = (modes[:, None] + 1) * (rows[None, :] + 1) % (2 * length + 2)
    return np.sqrt(2.0 / (length + 1)) * np.sin(np.pi * phase / (length + 1))


def sigma_of(length):
    return 4.0 * np.sin(np.pi * (np.arange(length) + 1.0) / (2.0 * length + 2.0)) ** 2


def time_tables(all_steps):
    slots = np.arange(all_steps // 2, dtype=np.int64)[:, None]
    moments = np.arange(all_steps, dtype=np.int64)[None, :]
    angle = 2.0 * np.pi / all_steps * (slots * moments % all_steps)
    parity = 1.0 - 2.0 * (moments % 2)
    first = slots == 0
    forward = np.concatenate([np.cos(angle), np.where(first, parity, -np.sin(angle))], 0)
    weight = np.where(first, 1.0, 2.0)
    inverse = np.concatenate(
        [weight * np.cos(angle), np.where(first, parity, -2.0 * np.sin(angle))], 0
    )
    rate = wrap_factor ** (np.arange(all_steps) / all_steps)
    return forward / rate[None, :], (inverse / all_steps).T * rate[:, None]


def matmul_2(left, right):
    a, b, c, d = left
    e, f, g, h = right
    return (a * e + b * g, a * f + b * h, c * e + d * g, c * f + d * h)


def power_2(base, count):
    result = None
    while count:
        if count & 1:
            result = base if result is None else matmul_2(result, base)
        count >>= 1
        if count:
            base = matmul_2(base, base)
    return result


def outgoing_kernel(steps, lines, r_ref, c_ref, o_ref):
    def chunk(i, carry):
        at = pl.ds(pl.multiple_of(i * lines, lines), lines)
        c = c_ref[at, :]
        ahead = jnp.zeros_like(c)
        further = jnp.zeros_like(c)
        for n in reversed(range(steps)):
            now = c * (r_ref[n, at, :] + (2.0 + damping) * ahead - further)
            ahead, further = now, ahead
        o_ref[0, at, :] = ahead
        o_ref[1, at, :] = further
        return carry

    lax.fori_loop(0, c_ref.shape[0] // lines, chunk, 0)


def march_kernel(steps, lines, r_ref, c_ref, s_ref, v_ref):
    def chunk(i, carry):
        at = pl.ds(pl.multiple_of(i * lines, lines), lines)
        c = c_ref[at, :]
        ahead = s_ref[0, at, :]
        further = s_ref[1, at, :]
        for n in reversed(range(steps)):
            now = c * (r_ref[n, at, :] + (2.0 + damping) * ahead - further)
            v_ref[n, at, :] = now
            ahead, further = now, ahead
        return carry

    lax.fori_loop(0, c_ref.shape[0] // lines, chunk, 0)


def in_vmem(count):
    return [pl.BlockSpec(memory_space=pltpu.VMEM)] * count


def outgoing(forced, mode_scale):
    steps, rows, cols = forced.shape
    return pl.pallas_call(
        functools.partial(outgoing_kernel, steps, 8),
        out_shape=jax.ShapeDtypeStruct((2, rows, cols), jnp.float32),
        in_specs=in_vmem(2),
        out_specs=in_vmem(1)[0],
        compiler_params=pltpu.CompilerParams(vmem_limit_bytes=32 * 2**20),
    )(forced, mode_scale)


def march(forced, mode_scale, state):
    steps, rows, cols = forced.shape
    return pl.pallas_call(
        functools.partial(march_kernel, steps, 8),
        out_shape=jax.ShapeDtypeStruct((steps, rows, cols), jnp.float32),
        in_specs=in_vmem(3),
        out_specs=in_vmem(1)[0],
        compiler_params=pltpu.CompilerParams(vmem_limit_bytes=32 * 2**20),
    )(forced, mode_scale, state)


def residual_kernel(steps, f_ref, a_ref, q_ref, next_ref, above_ref, below_ref, r_ref):
    rows, cols = q_ref.shape
    row = lax.broadcasted_iota(jnp.int32, (rows, cols), 0)
    col = lax.broadcasted_iota(jnp.int32, (rows, cols), 1)

    def one(n, later, latest):
        now = a_ref[n]
        w = q_ref[...] * now
        up = jnp.where(row == 0, above_ref[n], pltpu.roll(w, 1, 0))
        down = jnp.where(row == rows - 1, below_ref[n], pltpu.roll(w, rows - 1, 0))
        left = jnp.where(col == 0, 0.0, pltpu.roll(w, 1, 1))
        right = jnp.where(col == cols - 1, 0.0, pltpu.roll(w, cols - 1, 1))
        stiff = 4.0 * w - up - down - left - right
        applied = (1.0 + damping) * now - (2.0 + damping) * later + latest + stiff
        r_ref[n] = f_ref[n] - applied

    def step(n, carry):
        one(n, a_ref[n + 1], a_ref[n + 2])
        return carry

    lax.fori_loop(0, steps - 2, step, 0)
    one(steps - 2, a_ref[steps - 1], next_ref[0])
    one(steps - 1, next_ref[0], next_ref[1])


def residual(forcing, adjoint, speed_field, following, above, below):
    return pl.pallas_call(
        functools.partial(residual_kernel, forcing.shape[0]),
        out_shape=jax.ShapeDtypeStruct(forcing.shape, jnp.float32),
        in_specs=in_vmem(6),
        out_specs=in_vmem(1)[0],
        compiler_params=pltpu.CompilerParams(vmem_limit_bytes=40 * 2**20),
    )(forcing, adjoint, speed_field, following, above, below)


def f32(table):
    return jnp.asarray(np.asarray(table, np.float32))


def body(forcing, initial, class_map, speeds):
    steps, rows, cols = forcing.shape
    time_devices = lax.axis_size("ta")
    row_devices = lax.axis_size("gy")
    parts = time_devices * row_devices
    all_steps = steps * time_devices
    all_rows = rows * row_devices
    take = cols // parts
    slots = all_steps // 2
    edges = 2 * row_devices
    time_rank = lax.axis_index("ta")
    row_rank = lax.axis_index("gy")
    flat_rank = time_rank * row_devices + row_rank
    speed_sq = speeds * speeds
    mean_sq = jnp.mean(speed_sq)
    labels = jnp.arange(speeds.shape[0], dtype=jnp.int32)[:, None, None]
    speed_field = jnp.sum(
        jnp.where(class_map[None] == labels, speed_sq[:, None, None], 0.0), axis=0
    )

    x_table = f32(sine_rows(cols, np.arange(cols)))
    block_sine = sine_rows(rows, np.arange(rows))
    block_table = f32(block_sine)
    edge_modes = f32(block_sine[[0, rows - 1], :])
    forward, inverse = time_tables(all_steps)
    forward, inverse = f32(forward), f32(inverse)
    across = np.zeros((all_rows, row_devices, 2))
    whole = sine_rows(all_rows, np.arange(all_rows))
    for g in range(row_devices):
        if g > 0:
            across[:, g - 1, 1] = whole[:, g * rows]
        if g < row_devices - 1:
            across[:, g + 1, 0] = whole[:, (g + 1) * rows - 1]
    across = f32(across.reshape(all_rows, edges))

    mode_scale = 1.0 / (
        1.0 + damping + mean_sq * f32(sigma_of(rows)[:, None] + sigma_of(cols)[None, :])
    )
    one, none = jnp.ones_like(mode_scale), jnp.zeros_like(mode_scale)
    carried = power_2(((2.0 + damping) * mode_scale, -mode_scale, one, none), steps)
    round_trip = power_2(carried, time_devices)
    ra, rb, rc, rd = [wrap_factor * entry for entry in round_trip]
    det = (1.0 - ra) * (1.0 - rd) - rb * rc
    closing = ((1.0 - rd) / det, rb / det, rc / det, (1.0 - ra) / det)

    log_rate = np.log(wrap_factor) / all_steps
    factor = np.exp(log_rate)
    phase = 2.0 * np.pi / all_steps * np.arange(slots)
    wave_real = -np.expm1(log_rate) + 2.0 * factor * np.sin(0.5 * phase) ** 2
    wave_imag = -factor * np.sin(phase)
    base_real = np.repeat(
        wave_real * wave_real - wave_imag * wave_imag + damping * wave_real, take
    )
    base_imag = np.repeat(wave_imag * (2.0 * wave_real + damping), take)
    high = (1.0 + factor) ** 2 + damping * (1.0 + factor)
    col_index = (flat_rank * take + jnp.arange(take, dtype=jnp.int32)).astype(jnp.float32)
    col_sigma = 4.0 * jnp.sin(jnp.pi * (col_index + 1.0) / (2.0 * cols + 2.0)) ** 2
    col_sigma = jnp.tile(col_sigma, slots)
    spatial = mean_sq * (f32(sigma_of(all_rows))[:, None] + col_sigma[None, :])
    sym_real = f32(base_real)[None, :] + spatial
    sym_imag = f32(base_imag)[None, :]
    norm_sq = sym_real * sym_real + sym_imag * sym_imag
    scale_sq = mean_sq * mean_sq
    keep_real = scale_sq * sym_real / norm_sq
    cross = scale_sq * sym_imag / norm_sq
    is_first = jnp.arange(slots * take)[None, :] < take
    keep_imag = jnp.where(is_first, scale_sq / (high + spatial), keep_real)

    def incoming(out_state):
        parts_of = [
            lax.ppermute(
                out_state,
                "ta",
                [((i + by) % time_devices, i) for i in range(time_devices)],
            )
            for by in range(1, time_devices)
        ] + [out_state]
        a, b, c, d = carried
        first = second = None
        for i in reversed(range(time_devices)):
            place = time_rank + 1 + i
            weight = jnp.where(place >= time_devices, wrap_factor, 1.0)
            part = weight * parts_of[i]
            if first is None:
                first, second = part[0], part[1]
            else:
                first, second = part[0] + a * first + b * second, part[1] + c * first + d * second
        a, b, c, d = closing
        return jnp.stack([a * first + b * second, c * first + d * second])

    adjoint = initial
    for sweep in range(ITERS):
        following = passed_along(adjoint[:2], "ta", -1)
        above = passed_along(speed_field[-1:] * adjoint[:, -1:], "gy", 1)
        below = passed_along(speed_field[:1] * adjoint[:, :1], "gy", -1)
        resid = residual(forcing, adjoint, speed_field, following, above, below)
        x_modes = dot("ax,xj->aj", resid.reshape(-1, cols), x_table, MID).reshape(resid.shape)
        modes = dot("lp,npj->nlj", block_table, x_modes, MID)

        state = incoming(outgoing(modes, mode_scale))
        alone = march(modes, mode_scale, state)
        edge = dot("el,nlj->nej", edge_modes, alone, FINE)

        sent = edge.reshape(steps, 2, parts, take).transpose(2, 0, 1, 3).reshape(parts, -1)
        got = lax.all_to_all(sent, ("ta", "gy"), split_axis=0, concat_axis=0, tiled=True)
        got = got.reshape(time_devices, row_devices, steps, 2, take)
        got = got.transpose(0, 2, 1, 3, 4).reshape(all_steps, row_devices, 2, take)
        slotted = dot("kn,na->ka", forward, got.reshape(all_steps, -1), FINE)
        slotted = slotted.reshape(2 * slots, edges, take).transpose(1, 0, 2)
        rowed = dot("le,ea->la", across, slotted.reshape(edges, -1), FINE)
        row_real, row_imag = rowed[:, : slots * take], rowed[:, slots * take :]
        div = jnp.concatenate(
            [row_real * keep_real + row_imag * cross, row_imag * keep_imag - row_real * cross],
            axis=1,
        )
        back = dot("le,la->ea", across, div, FINE)
        back = back.reshape(edges, 2 * slots, take).transpose(1, 0, 2).reshape(2 * slots, -1)
        change = dot("nk,ka->na", inverse, back, FINE).reshape(got.shape)
        blank = jnp.zeros_like(got[:, :1, 0])
        beside = jnp.stack(
            [
                jnp.concatenate([blank, got[:, :-1, 1]], axis=1),
                jnp.concatenate([got[:, 1:, 0], blank], axis=1),
            ],
            axis=2,
        )
        coupled = mean_sq * beside + change
        sent = coupled.reshape(time_devices, steps, row_devices, 2, take)
        sent = sent.transpose(0, 2, 1, 3, 4).reshape(parts, -1)
        got = lax.all_to_all(sent, ("ta", "gy"), split_axis=0, concat_axis=0, tiled=True)
        coupled = got.reshape(parts, steps, 2, take).transpose(1, 2, 0, 3).reshape(steps, 2, cols)

        modes = modes + dot("el,nej->nlj", edge_modes, coupled, FINE)
        state = incoming(outgoing(modes, mode_scale))
        solved = march(modes, mode_scale, state)
        solved = dot("lp,nlj->npj", block_table, solved, MID)
        correction = dot("aj,jx->ax", solved.reshape(-1, cols), x_table, MID)
        adjoint = adjoint + correction.reshape(adjoint.shape)
    return adjoint


def solution(mesh):
    return jax.shard_map(
        body,
        mesh=mesh,
        in_specs=(P("ta", "gy", None), P("ta", "gy", None), P("gy", None), P()),
        out_specs=P("ta", "gy", None),
        check_vma=False,
    )
```

```python
import functools

import jax
import jax.numpy as jnp
import numpy as np
from jax import lax
from jax.experimental import pallas as pl
from jax.experimental.pallas import tpu as pltpu
from jax.sharding import PartitionSpec as P

ITERS = 2


damping = 0.2
wrap_factor = 0.01
FINE = lax.Precision.HIGHEST
MID = lax.Precision.HIGH


def dot(subscripts, left, right, precision):
    return jnp.einsum(
        subscripts, left, right, precision=precision, preferred_element_type=jnp.float32
    )


def passed_along(value, axis, by):
    length = lax.axis_size(axis)
    pairs = [(i, i + by) for i in range(length) if 0 <= i + by < length]
    return lax.ppermute(value, axis, pairs)


def sine_rows(length, rows):
    modes = np.arange(length, dtype=np.int64)
    phase = (modes[:, None] + 1) * (rows[None, :] + 1) % (2 * length + 2)
    return np.sqrt(2.0 / (length + 1)) * np.sin(np.pi * phase / (length + 1))


def sigma_of(length):
    return 4.0 * np.sin(np.pi * (np.arange(length) + 1.0) / (2.0 * length + 2.0)) ** 2


def time_tables(all_steps):
    slots = np.arange(all_steps // 2, dtype=np.int64)[:, None]
    moments = np.arange(all_steps, dtype=np.int64)[None, :]
    angle = 2.0 * np.pi / all_steps * (slots * moments % all_steps)
    parity = 1.0 - 2.0 * (moments % 2)
    first = slots == 0
    forward = np.concatenate([np.cos(angle), np.where(first, parity, -np.sin(angle))], 0)
    weight = np.where(first, 1.0, 2.0)
    inverse = np.concatenate(
        [weight * np.cos(angle), np.where(first, parity, -2.0 * np.sin(angle))], 0
    )
    rate = wrap_factor ** (np.arange(all_steps) / all_steps)
    return forward / rate[None, :], (inverse / all_steps).T * rate[:, None]


def matmul_2(left, right):
    a, b, c, d = left
    e, f, g, h = right
    return (a * e + b * g, a * f + b * h, c * e + d * g, c * f + d * h)


def power_2(base, count):
    result = None
    while count:
        if count & 1:
            result = base if result is None else matmul_2(result, base)
        count >>= 1
        if count:
            base = matmul_2(base, base)
    return result


def outgoing_kernel(steps, lines, r_ref, c_ref, o_ref):
    def chunk(i, carry):
        at = pl.ds(pl.multiple_of(i * lines, lines), lines)
        c = c_ref[at, :]
        ahead = jnp.zeros_like(c)
        further = jnp.zeros_like(c)
        for n in reversed(range(steps)):
            now = c * (r_ref[n, at, :] + (2.0 + damping) * ahead - further)
            ahead, further = now, ahead
        o_ref[0, at, :] = ahead
        o_ref[1, at, :] = further
        return carry

    lax.fori_loop(0, c_ref.shape[0] // lines, chunk, 0)


def march_kernel(steps, lines, r_ref, c_ref, s_ref, v_ref):
    def chunk(i, carry):
        at = pl.ds(pl.multiple_of(i * lines, lines), lines)
        c = c_ref[at, :]
        ahead = s_ref[0, at, :]
        further = s_ref[1, at, :]
        for n in reversed(range(steps)):
            now = c * (r_ref[n, at, :] + (2.0 + damping) * ahead - further)
            v_ref[n, at, :] = now
            ahead, further = now, ahead
        return carry

    lax.fori_loop(0, c_ref.shape[0] // lines, chunk, 0)


def in_vmem(count):
    return [pl.BlockSpec(memory_space=pltpu.VMEM)] * count


def outgoing(forced, mode_scale):
    steps, rows, cols = forced.shape
    return pl.pallas_call(
        functools.partial(outgoing_kernel, steps, 8),
        out_shape=jax.ShapeDtypeStruct((2, rows, cols), jnp.float32),
        in_specs=in_vmem(2),
        out_specs=in_vmem(1)[0],
        compiler_params=pltpu.CompilerParams(vmem_limit_bytes=32 * 2**20),
    )(forced, mode_scale)


def march(forced, mode_scale, state):
    steps, rows, cols = forced.shape
    return pl.pallas_call(
        functools.partial(march_kernel, steps, 8),
        out_shape=jax.ShapeDtypeStruct((steps, rows, cols), jnp.float32),
        in_specs=in_vmem(3),
        out_specs=in_vmem(1)[0],
        compiler_params=pltpu.CompilerParams(vmem_limit_bytes=32 * 2**20),
    )(forced, mode_scale, state)


def residual_kernel(steps, f_ref, a_ref, q_ref, next_ref, above_ref, below_ref, r_ref):
    rows, cols = q_ref.shape
    row = lax.broadcasted_iota(jnp.int32, (rows, cols), 0)
    col = lax.broadcasted_iota(jnp.int32, (rows, cols), 1)

    def one(n, later, latest):
        now = a_ref[n]
        w = q_ref[...] * now
        up = jnp.where(row == 0, above_ref[n], pltpu.roll(w, 1, 0))
        down = jnp.where(row == rows - 1, below_ref[n], pltpu.roll(w, rows - 1, 0))
        left = jnp.where(col == 0, 0.0, pltpu.roll(w, 1, 1))
        right = jnp.where(col == cols - 1, 0.0, pltpu.roll(w, cols - 1, 1))
        stiff = 4.0 * w - up - down - left - right
        applied = (1.0 + damping) * now - (2.0 + damping) * later + latest + stiff
        r_ref[n] = f_ref[n] - applied

    def step(n, carry):
        one(n, a_ref[n + 1], a_ref[n + 2])
        return carry

    lax.fori_loop(0, steps - 2, step, 0)
    one(steps - 2, a_ref[steps - 1], next_ref[0])
    one(steps - 1, next_ref[0], next_ref[1])


def residual(forcing, adjoint, speed_field, following, above, below):
    return pl.pallas_call(
        functools.partial(residual_kernel, forcing.shape[0]),
        out_shape=jax.ShapeDtypeStruct(forcing.shape, jnp.float32),
        in_specs=in_vmem(6),
        out_specs=in_vmem(1)[0],
        compiler_params=pltpu.CompilerParams(vmem_limit_bytes=40 * 2**20),
    )(forcing, adjoint, speed_field, following, above, below)


def f32(table):
    return jnp.asarray(np.asarray(table, np.float32))


def body(forcing, initial, class_map, speeds):
    steps, rows, cols = forcing.shape
    time_devices = lax.axis_size("ta")
    row_devices = lax.axis_size("gy")
    parts = time_devices * row_devices
    all_steps = steps * time_devices
    all_rows = rows * row_devices
    take = cols // parts
    slots = all_steps // 2
    edges = 2 * row_devices
    time_rank = lax.axis_index("ta")
    row_rank = lax.axis_index("gy")
    flat_rank = time_rank * row_devices + row_rank
    speed_sq = speeds * speeds
    mean_sq = jnp.mean(speed_sq)
    labels = jnp.arange(speeds.shape[0], dtype=jnp.int32)[:, None, None]
    speed_field = jnp.sum(
        jnp.where(class_map[None] == labels, speed_sq[:, None, None], 0.0), axis=0
    )

    x_table = f32(sine_rows(cols, np.arange(cols)))
    block_sine = sine_rows(rows, np.arange(rows))
    block_table = f32(block_sine)
    edge_modes = f32(block_sine[[0, rows - 1], :])
    forward, inverse = time_tables(all_steps)
    forward, inverse = f32(forward), f32(inverse)
    across = np.zeros((all_rows, row_devices, 2))
    whole = sine_rows(all_rows, np.arange(all_rows))
    for g in range(row_devices):
        if g > 0:
            across[:, g - 1, 1] = whole[:, g * rows]
        if g < row_devices - 1:
            across[:, g + 1, 0] = whole[:, (g + 1) * rows - 1]
    across = f32(across.reshape(all_rows, edges))

    mode_scale = 1.0 / (
        1.0 + damping + mean_sq * f32(sigma_of(rows)[:, None] + sigma_of(cols)[None, :])
    )
    one, none = jnp.ones_like(mode_scale), jnp.zeros_like(mode_scale)
    carried = power_2(((2.0 + damping) * mode_scale, -mode_scale, one, none), steps)
    round_trip = power_2(carried, time_devices)
    ra, rb, rc, rd = [wrap_factor * entry for entry in round_trip]
    det = (1.0 - ra) * (1.0 - rd) - rb * rc
    closing = ((1.0 - rd) / det, rb / det, rc / det, (1.0 - ra) / det)

    log_rate = np.log(wrap_factor) / all_steps
    factor = np.exp(log_rate)
    phase = 2.0 * np.pi / all_steps * np.arange(slots)
    wave_real = -np.expm1(log_rate) + 2.0 * factor * np.sin(0.5 * phase) ** 2
    wave_imag = -factor * np.sin(phase)
    base_real = np.repeat(
        wave_real * wave_real - wave_imag * wave_imag + damping * wave_real, take
    )
    base_imag = np.repeat(wave_imag * (2.0 * wave_real + damping), take)
    high = (1.0 + factor) ** 2 + damping * (1.0 + factor)
    col_index = (flat_rank * take + jnp.arange(take, dtype=jnp.int32)).astype(jnp.float32)
    col_sigma = 4.0 * jnp.sin(jnp.pi * (col_index + 1.0) / (2.0 * cols + 2.0)) ** 2
    col_sigma = jnp.tile(col_sigma, slots)
    spatial = mean_sq * (f32(sigma_of(all_rows))[:, None] + col_sigma[None, :])
    sym_real = f32(base_real)[None, :] + spatial
    sym_imag = f32(base_imag)[None, :]
    norm_sq = sym_real * sym_real + sym_imag * sym_imag
    scale_sq = mean_sq * mean_sq
    keep_real = scale_sq * sym_real / norm_sq
    cross = scale_sq * sym_imag / norm_sq
    is_first = jnp.arange(slots * take)[None, :] < take
    keep_imag = jnp.where(is_first, scale_sq / (high + spatial), keep_real)

    def incoming(out_state):
        parts_of = [
            lax.ppermute(
                out_state,
                "ta",
                [((i + by) % time_devices, i) for i in range(time_devices)],
            )
            for by in range(1, time_devices)
        ] + [out_state]
        a, b, c, d = carried
        first = second = None
        for i in reversed(range(time_devices)):
            place = time_rank + 1 + i
            weight = jnp.where(place >= time_devices, wrap_factor, 1.0)
            part = weight * parts_of[i]
            if first is None:
                first, second = part[0], part[1]
            else:
                first, second = part[0] + a * first + b * second, part[1] + c * first + d * second
        a, b, c, d = closing
        return jnp.stack([a * first + b * second, c * first + d * second])

    adjoint = initial
    for sweep in range(ITERS):
        following = passed_along(adjoint[:2], "ta", -1)
        above = passed_along(speed_field[-1:] * adjoint[:, -1:], "gy", 1)
        below = passed_along(speed_field[:1] * adjoint[:, :1], "gy", -1)
        resid = residual(forcing, adjoint, speed_field, following, above, below)
        x_modes = dot("ax,xj->aj", resid.reshape(-1, cols), x_table, MID).reshape(resid.shape)
        modes = dot("lp,npj->nlj", block_table, x_modes, MID)

        state = incoming(outgoing(modes, mode_scale))
        alone = march(modes, mode_scale, state)
        edge = dot("el,nlj->nej", edge_modes, alone, FINE)

        sent = edge.reshape(steps, 2, parts, take).transpose(2, 0, 1, 3).reshape(parts, -1)
        got = lax.all_to_all(sent, ("ta", "gy"), split_axis=0, concat_axis=0, tiled=True)
        got = got.reshape(time_devices, row_devices, steps, 2, take)
        got = got.transpose(0, 2, 1, 3, 4).reshape(all_steps, row_devices, 2, take)
        slotted = dot("kn,na->ka", forward, got.reshape(all_steps, -1), FINE)
        slotted = slotted.reshape(2 * slots, edges, take).transpose(1, 0, 2)
        rowed = dot("le,ea->la", across, slotted.reshape(edges, -1), FINE)
        row_real, row_imag = rowed[:, : slots * take], rowed[:, slots * take :]
        div = jnp.concatenate(
            [row_real * keep_real + row_imag * cross, row_imag * keep_imag - row_real * cross],
            axis=1,
        )
        back = dot("le,la->ea", across, div, FINE)
        back = back.reshape(edges, 2 * slots, take).transpose(1, 0, 2).reshape(2 * slots, -1)
        change = dot("nk,ka->na", inverse, back, FINE).reshape(got.shape)
        blank = jnp.zeros_like(got[:, :1, 0])
        beside = jnp.stack(
            [
                jnp.concatenate([blank, got[:, :-1, 1]], axis=1),
                jnp.concatenate([got[:, 1:, 0], blank], axis=1),
            ],
            axis=2,
        )
        coupled = mean_sq * beside + change
        sent = coupled.reshape(time_devices, steps, row_devices, 2, take)
        sent = sent.transpose(0, 2, 1, 3, 4).reshape(parts, -1)
        got = lax.all_to_all(sent, ("ta", "gy"), split_axis=0, concat_axis=0, tiled=True)
        coupled = got.reshape(parts, steps, 2, take).transpose(1, 2, 0, 3).reshape(steps, 2, cols)

        low, top = edge_modes[0][None, :, None], edge_modes[1][None, :, None]
        modes = modes + low * coupled[:, :1] + top * coupled[:, 1:]
        state = incoming(outgoing(modes, mode_scale))
        solved = march(modes, mode_scale, state)
        solved = dot("lp,nlj->npj", block_table, solved, MID)
        correction = dot("aj,jx->ax", solved.reshape(-1, cols), x_table, MID)
        adjoint = adjoint + correction.reshape(adjoint.shape)
    return adjoint


def solution(mesh):
    return jax.shard_map(
        body,
        mesh=mesh,
        in_specs=(P("ta", "gy", None), P("ta", "gy", None), P("gy", None), P()),
        out_specs=P("ta", "gy", None),
        check_vma=False,
    )
```
